1024 devices in a mesh: row: 32 (over x, y), col: 32 (over z, core).
Axes of the slice: x: 4, y: 8, z: 16, core: 2. Of those that a mesh axis runs over, the one named last changes fastest.
Arguments:
- amp_cycle: float32 [4096, 64, 128], P(('row', 'col')), may hold values from -6 to 6
- cycle_ints: float32 [32768, 2, 64, 64], P(('row', 'col')), may hold values from -0.5 to 0.5
- cycle_refs: int32 [32768, 2], P(('row', 'col')), may hold values from 0 to 31, as said below
- wanted: int32 [1024, 32, 1], P(('row', 'col')), may hold values from 0 to 3, as said below
- cycle_dest: int32 [32768], P(('row', 'col')), may hold values from 0 to 1023, as said below
- ladder_ints: float32 [8192, 64, 64], P(('row', 'col')), may hold values from -0.5 to 0.5
- ladder_amps: float32 [8192, 64, 128], P(('row', 'col')), may hold values from -6 to 6
- ladder_int_ref: int32 [32768, 2], P(('row', 'col')), may hold values from 0 to 7
- ladder_amp_ref: int32 [32768, 2], P(('row', 'col')), may hold values from 0 to 7
Outputs:
- residual: float32 [32768, 64, 128], P(('row', 'col'))
The draws below stay inside these ranges and needn't reach their ends.
Inputs may be any that keep to these rules, and one draw needn't show every extreme that they name: `cycle_refs`: within one device's cycle tiles, every value 0 to 31 appears exactly 32 * 2 / 32 times. For each device and each h, the 1 entries wanted[d, h, :] are distinct. Each device sends exactly 1 of its cycle tiles to each index of row (cycle_dest // 32), and within each column group every ladder tile receives exactly one cycle tile.
All inputs are finite; a program needn't handle non-finite values.
Results may differ from the reference program's by a relative error of at most 0.0003.
Values sent between devices are 32-bit elements; how exact they have to be, the bound alone decides.
A program may use at most 32 MiB of HBM per device.

```python
import jax
import jax.numpy as jnp
from jax import lax

TILE = 64
SLAB = 128
XP = 1
KP = 4
CAPR = 1
NZ = 2
LP = 8
LA = 8
NZL = 2
RT = 32
OVT = 32768
POOL = 4096
LPOOL = 8192
APOOL = 8192
N_ROW = 32
N_COL = 32


def draw_cycle_refs(key, part):
    key = jax.random.fold_in(key, 11)
    count = XP * N_ROW * NZ
    scores = jax.random.randint(key, (N_ROW * N_COL, count), 0, 1 << 16) * count + jnp.arange(count, dtype=jnp.int32)
    shuffled = jnp.argsort(scores, axis=-1).astype(jnp.int32)
    picks = shuffled % (N_COL * CAPR)
    return picks.reshape(N_ROW * N_COL * XP * N_ROW, NZ).astype(jnp.int32)


def draw_wanted(key, part):
    key = jax.random.fold_in(key, 12)
    scores = jax.random.randint(key, (N_ROW * N_COL, N_COL, KP), 0, 1 << 16) * KP + jnp.arange(KP, dtype=jnp.int32)
    shuffled = jnp.argsort(scores, axis=-1).astype(jnp.int32)
    return shuffled[:, :, :CAPR].astype(jnp.int32)


def draw_cycle_dest(key, part):
    key = jax.random.fold_in(key, 13)
    first_key, second_key = jax.random.split(key)
    count = XP * N_ROW
    first_scores = jax.random.randint(first_key, (N_COL, N_ROW, count), 0, 1 << 16) * count + jnp.arange(count, dtype=jnp.int32)
    outgoing = jnp.argsort(first_scores, axis=-1).astype(jnp.int32)
    dest_row = outgoing // XP
    within = outgoing % XP
    second_scores = jax.random.randint(second_key, (N_COL, N_ROW, count), 0, 1 << 16) * count + jnp.arange(count, dtype=jnp.int32)
    arrival = jnp.argsort(second_scores, axis=-1).astype(jnp.int32)
    incoming = jnp.arange(N_ROW, dtype=jnp.int32)[None, :, None] * XP + within
    flat_index = (dest_row * count + incoming).reshape(N_COL, N_ROW * count)
    slots = jnp.take_along_axis(arrival.reshape(N_COL, N_ROW * count), flat_index, axis=1).reshape(N_COL, N_ROW, count)
    values = dest_row * count + slots
    return jnp.transpose(values, (1, 0, 2)).reshape(N_ROW * N_COL * count).astype(jnp.int32)


def set_ends(drawn, key, low, high):
    extent = drawn.shape
    spot = [jax.random.randint(jax.random.fold_in(key, axis), (), 0, extent[axis]) for axis in range(len(extent))]
    drawn = drawn.at[tuple(spot)].set(low)
    longest = extent.index(max(extent))
    spot[longest] = (spot[longest] + 1) % extent[longest]
    return drawn.at[tuple(spot)].set(high)


def levels(stream_key, extent, cuts, smallest, top_value):
    def one(dim, shards_of):
        steps = jax.random.uniform(jax.random.fold_in(jax.random.fold_in(stream_key, 6), dim), (shards_of,), jnp.float32, smallest / len(cuts), top_value / len(cuts))
        return jnp.repeat(jnp.exp(steps), extent[dim] // shards_of).reshape((-1,) + (1,) * (len(extent) - dim - 1))

    gain = one(*cuts[0])
    for cut in cuts[1:]:
        gain = gain * one(*cut)
    return gain


def centred(rng, dims, deviation, bound, cuts=(), held_as=jnp.bfloat16):
    loudness = levels(rng, dims, cuts, -0.22, 0.18) if cuts else 1.0
    drawn = jax.random.normal(rng, dims, jnp.float32) * deviation * loudness
    return jnp.minimum(jnp.maximum(drawn, -bound), bound).astype(held_as)


def setup_inputs(seed: int = 0) -> dict:
    splits = jax.random.split(jax.random.key(seed), 10)
    return {
        "amp_cycle": centred(splits[0], (POOL, TILE, SLAB), 1.0, 6.0, ((0, 1024),), jnp.float32),
        "cycle_ints": centred(splits[1], (OVT, NZ, TILE, TILE), (TILE * NZ) ** -0.5, 0.5, ((0, 1024),), jnp.float32),
        "cycle_refs": draw_cycle_refs(jax.random.fold_in(splits[9], 71), 0),
        "wanted": draw_wanted(jax.random.fold_in(splits[9], 71), 0),
        "cycle_dest": draw_cycle_dest(jax.random.fold_in(splits[9], 71), 0),
        "ladder_ints": centred(splits[5], (LPOOL, TILE, TILE), (TILE * NZL) ** -0.5, 0.5, ((0, 1024),), jnp.float32),
        "ladder_amps": centred(splits[6], (APOOL, TILE, SLAB), 1.0, 6.0, ((0, 1024),), jnp.float32),
        "ladder_int_ref": set_ends(jax.random.randint(splits[7], (OVT, NZL), 0, LP), jax.random.fold_in(splits[7], 1), 0, LP - 1).astype(jnp.int32),
        "ladder_amp_ref": set_ends(jax.random.randint(splits[8], (OVT, NZL), 0, LA), jax.random.fold_in(splits[8], 1), 0, LA - 1).astype(jnp.int32),
    }


def reference(amp_cycle, cycle_ints, cycle_refs, wanted, cycle_dest, ladder_ints, ladder_amps, ladder_int_ref, ladder_amp_ref):
    highest = lax.Precision.HIGHEST
    device_count = N_ROW * N_COL

    def cycle_block(index):
        row_index = index // N_COL
        block_ints = lax.dynamic_slice_in_dim(cycle_ints, index * RT, RT, 0)
        block_refs = lax.dynamic_slice_in_dim(cycle_refs, index * RT, RT, 0)
        block_want = lax.dynamic_index_in_dim(wanted, index, 0, keepdims=False)
        holders = jnp.arange(N_COL, dtype=jnp.int32)[:, None]
        lookup = ((row_index * N_COL + holders) * KP + block_want).reshape(-1)
        sources = amp_cycle[lookup[block_refs]]
        return jnp.einsum("tsij,tsjk->tik", block_ints, sources, precision=highest)

    def ladder_block(index):
        int_refs = lax.dynamic_slice_in_dim(ladder_int_ref, index * RT, RT, 0)
        amp_refs = lax.dynamic_slice_in_dim(ladder_amp_ref, index * RT, RT, 0)
        block_ints = ladder_ints[index * LP + int_refs]
        block_amps = ladder_amps[index * LA + amp_refs]
        return jnp.einsum("tmij,tmjk->tik", block_ints, block_amps, precision=highest)

    indices = jnp.arange(device_count, dtype=jnp.int32)
    cycle_all = lax.map(cycle_block, indices).reshape(OVT, TILE, SLAB)
    ladder_all = lax.map(ladder_block, indices).reshape(OVT, TILE, SLAB)
    tile_index = jnp.arange(OVT, dtype=jnp.int32)
    column = (tile_index // RT) % N_COL
    target = ((cycle_dest // RT) * N_COL + column) * RT + cycle_dest % RT
    return ladder_all.at[target].add(cycle_all)
```

```python
import functools

import jax
import jax.numpy as jnp
from jax import lax
from jax.experimental import pallas as pl
from jax.experimental.pallas import tpu as pltpu
from jax.sharding import PartitionSpec as P

MESH = pl.DeviceIdType.MESH
NX, NY, NZ, NCORE = 4, 8, 16, 2
NQ = 4
NEAR = {1: 0, 2: 1, 3: 0, 4: 3, 5: 4, 6: 3, 7: 6, 8: 6}
RING = {m: m - 1 for m in range(1, 9)}
TREES = (NEAR, NEAR, RING, RING)
NEAR_AT = {1: 3.5, 3: 5.5, 2: 7.0, 4: 9.0, 6: 11.0, 5: 12.5, 7: 14.5, 8: 15.5}
RING_AT = {m: 3.6 * m for m in range(1, 9)}
START = (0.0, 0.01, 0.02, 0.03)
DELAY = (0.0, 6.0, 1.0, 2.0)
PIECE = 1.2
ORDER = (4, 3, 5, 2, 6, 1, 7, 0)


def shifted(value, blocks):
    amount = (blocks * 32) % 128
    return value if amount == 0 else pltpu.roll(value, amount, axis=1)


def pick(lane_block, choices):
    out = choices[0]
    for p in range(1, 4):
        out = jnp.where(lane_block == p, choices[p], out)
    return out


def split(value):
    high = value.astype(jnp.bfloat16)
    low = (value - high.astype(jnp.float32)).astype(jnp.bfloat16)
    return high, low


def kernel(
    amp_hbm,
    ints_hbm,
    refs_hbm,
    wanted_hbm,
    dest_hbm,
    lint_hbm,
    lamp_hbm,
    int_ref_hbm,
    amp_ref_hbm,
    out,
    refs,
    wanted,
    dest,
    int_ref,
    amp_ref,
    amp,
    ints,
    lint,
    lamp,
    held_0,
    held_1,
    held_2,
    held_3,
    lhs,
    going,
    came_0,
    came_1,
    came_2,
    came_3,
    passed,
    pair,
    dest_col,
    slot_row,
    slots,
    table,
    inverse,
    origin,
    place,
    which,
    load_sem,
    table_sem,
    ring_sem,
    ring_sent,
    twin_sem,
    relay_sem,
    slot_sem,
    slot_sent,
    row_sem,
    row_sent,
):
    came = (came_0, came_1, came_2, came_3)
    held = (held_0, held_1, held_2, held_3)
    row, col = lax.axis_index("row"), lax.axis_index("col")
    x, y = row // NY, row % NY
    z, core = col // NCORE, col % NCORE
    way = 1 - 2 * core
    mate = 1 - core

    def along(links, to_core):
        return (row, ((z + way * links + NZ) % NZ) * NCORE + to_core)

    twin = along(0, mate)

    def peer_row(k):
        return ((x + k % NX) % NX) * NY + (y + k // NX) % NY

    loads = [
        pltpu.make_async_copy(a, b, load_sem.at[i])
        for i, (a, b) in enumerate(
            (
                (amp_hbm, amp),
                (dest_hbm, dest),
                (refs_hbm, refs),
                (wanted_hbm, wanted),
                (ints_hbm, ints),
                (lint_hbm, lint),
                (lamp_hbm, lamp),
                (int_ref_hbm, int_ref),
                (amp_ref_hbm, amp_ref),
            )
        )
    ]
    for load in loads:
        load.start()

    barrier = pltpu.get_barrier_semaphore()
    senders = (
        along(-1, core),
        along(-2, core),
        along(-3, core),
        along(-1, mate),
        along(-3, mate),
        twin,
    )
    for device in senders:
        pl.semaphore_signal(barrier, inc=1, device_id=device, device_id_type=MESH)

    def greet(k, carry):
        pl.semaphore_signal(barrier, inc=1, device_id=(peer_row(k), col), device_id_type=MESH)
        return carry

    lax.fori_loop(1, 32, greet, 0)

    lane_block = lax.broadcasted_iota(jnp.int32, (16, 128), 1) // 32

    loads[0].wait()
    for w in range(4):
        skewed = [shifted(amp[w, 16 * a : 16 * a + 16, :], a) for a in range(4)]
        for q in range(NQ):
            held[q][core, w] = pick(lane_block, [skewed[(p - q) % 4] for p in range(4)])

    loads[1].wait()
    for t in range(32):
        dest_col[t : t + 1, :] = jnp.full((1, 128), dest[t], jnp.int32)
    lane = lax.broadcasted_iota(jnp.int32, (32, 128), 1)
    sub = lax.broadcasted_iota(jnp.int32, (32, 128), 0)
    goal = dest_col[...]
    to_row = (goal // 32) == lane
    table[0:1, :] = jnp.max(jnp.where(to_row, sub, 0), axis=0, keepdims=True)
    slot = jnp.max(jnp.where(to_row, goal % 32, 0), axis=0, keepdims=True)
    slot_row[...] = slot
    slots[0:1, :] = slot
    invert = pltpu.make_async_copy(table.at[0:1], inverse, table_sem)
    invert.start()

    pl.semaphore_wait(barrier, len(senders) + 31)

    def send(q, source, target, device, semaphore, sent=0):
        pltpu.make_async_remote_copy(
            src_ref=held[q].at[source],
            dst_ref=held[q].at[target],
            send_sem=ring_sent.at[q, sent],
            recv_sem=semaphore,
            device_id=device,
            device_id_type=MESH,
        ).start()

    def await_block(q, block, semaphore):
        ref = held[q].at[block]
        pltpu.make_async_copy(ref, ref, semaphore).wait()

    def blocks(first, last):
        return pl.ds(2 * first, 2 * (last - first))

    def onward(q, m):
        return sorted((n for n in TREES[q] if TREES[q][n] == m), reverse=True)

    def inject(q):
        for n in onward(q, 0):
            send(q, core, 2 * n + core, along(n, core), ring_sem.at[q, n, core])
            send(q, core, 2 * n + core, along(-n, mate), ring_sem.at[q, n, core])
        send(q, core, core, twin, twin_sem.at[q, 0], sent=1)

    def hop(q, m):
        if TREES[q][m] == 0:
            for c in range(NCORE):
                await_block(q, 2 * m + c, ring_sem.at[q, m, c])
        elif m < 8:
            await_block(q, blocks(m, m + 1), ring_sem.at[q, m, 0])
        else:
            await_block(q, 16 + core, ring_sem.at[q, 8, 0])
        for n in onward(q, m):
            if n == 8:
                send(q, 2 * m + core, 16 + core, along(8 - m, core), ring_sem.at[q, 8, 0])
            else:
                send(q, blocks(m, m + 1), blocks(n, n + 1), along(n - m, core), ring_sem.at[q, n, 0])
        if m == 8:
            send(q, 16 + core, 34 + core, twin, twin_sem.at[q, 2], sent=3)
        else:
            send(q, blocks(m, m + 1), blocks(m + 9, m + 10), twin, twin_sem.at[q, 1], sent=2)

    def others(q):
        await_block(q, mate, twin_sem.at[q, 0])
        await_block(q, blocks(10, 17), twin_sem.at[q, 1])
        await_block(q, 34 + mate, twin_sem.at[q, 2])

    def send_slots():
        def one(k, carry):
            pltpu.make_async_remote_copy(
                src_ref=slot_row,
                dst_ref=slots.at[pl.ds(k, 1)],
                send_sem=slot_sent,
                recv_sem=slot_sem,
                device_id=(peer_row(k), col),
                device_id_type=MESH,
            ).start()
            return carry

        lax.fori_loop(1, 32, one, 0)

    def indices():
        invert.wait()
        loads[2].wait()
        loads[3].wait()

        def one(k, carry):
            t = inverse[0, peer_row(k)]
            for s in range(2):
                h = refs[s, t]
                m = (way * (z - h // 2) + 2 * NZ) % NZ
                own = jnp.logical_or(m < 8, jnp.logical_and(m == 8, h % 2 == core))
                place[2 * k + s] = jnp.where(own, 2 * m, 18 + 2 * (NZ - m)) + h % 2
                which[2 * k + s] = wanted[0, h]
            return carry

        lax.fori_loop(0, 32, one, 0, unroll=4)

    def prepare_ints():
        loads[4].wait()

        def one(k, carry):
            t = inverse[0, peer_row(k)]
            both = jnp.concatenate([ints[t, 0], ints[t, 1]], axis=1)
            high, low = split(both)
            lhs[k] = jnp.concatenate([high, low], axis=1)
            return carry

        lax.fori_loop(0, 32, one, 0, unroll=4)

    def ladder_pairs():
        loads[5].wait()
        loads[6].wait()
        ih, il = split(lint[...].reshape(512, 64))
        left = jnp.concatenate([ih, il, ih], axis=1)

        def one(b, carry):
            high, low = split(lamp[b])
            right = jnp.concatenate([high, high, low], axis=0)
            product = jnp.dot(left, right, preferred_element_type=jnp.float32)
            pair[b] = product.reshape(8, 64, 128)
            return carry

        lax.fori_loop(0, 8, one, 0, unroll=2)

    def arrivals():
        pltpu.make_async_copy(slots.at[1:32], slots.at[1:32], slot_sem).wait()
        mine = jnp.max(jnp.where(lane == row, slots[...], 0), axis=1, keepdims=True)
        table[1:2, :] = jnp.max(jnp.where(mine == lane, sub, 0), axis=0, keepdims=True)
        copy = pltpu.make_async_copy(table.at[1:2], origin, table_sem)
        copy.start()
        copy.wait()

    def chunk_products(q, i):
        rows = []
        for s in range(2):
            turned = [
                shifted(held[q][place[8 * i + 2 * e + s], which[8 * i + 2 * e + s]], e)
                for e in range(4)
            ]
            for a in range(4):
                mixed = pick(lane_block, [turned[(p - a - q) % 4] for p in range(4)])
                rows.append(shifted(mixed, -a - q))
        high, low = split(jnp.concatenate(rows, axis=0))
        left = lhs[pl.ds(4 * i, 4)].reshape(256, 256)
        product = jnp.dot(
            left, jnp.concatenate([high, high], axis=0), preferred_element_type=jnp.float32
        ) + jnp.dot(left[:, :128], low, preferred_element_type=jnp.float32)
        for e in range(4):
            parts = [
                shifted(product[64 * e + 16 * a : 64 * e + 16 * a + 16, :], a) for a in range(4)
            ]
            mixed = pick(lane_block, [parts[(p - e) % 4] for p in range(4)])
            going[4 * i + e, q] = shifted(mixed, q - e)

    def row_send(q, k):
        pltpu.make_async_remote_copy(
            src_ref=going.at[k, q],
            dst_ref=came[q].at[k],
            send_sem=row_sent.at[q],
            recv_sem=row_sem.at[q],
            device_id=(peer_row(k), col),
            device_id_type=MESH,
        ).start()

    def relay_copy(q):
        return pltpu.make_async_remote_copy(
            src_ref=going.at[16:20, q],
            dst_ref=passed.at[q],
            send_sem=relay_sem.at[q, 0],
            recv_sem=relay_sem.at[q, 1],
            device_id=(x * NY + (y + NY - 1) % NY, col),
            device_id_type=MESH,
        )

    def relay(q):
        @pl.when(core == 1)
        def _():
            relay_copy(q).wait_recv()
            for dx in range(NX):
                pltpu.make_async_remote_copy(
                    src_ref=passed.at[q, dx],
                    dst_ref=came[q].at[16 + dx],
                    send_sem=relay_sem.at[q, 2],
                    recv_sem=row_sem.at[q],
                    device_id=(peer_row(20 + dx), col),
                    device_id_type=MESH,
                ).start()

    def products(q, piece):
        for i in ORDER[2 * piece : 2 * piece + 2]:
            chunk_products(q, i)
        for i in ORDER[2 * piece : 2 * piece + 2]:
            if i == 4:

                @pl.when(core == 0)
                def _():
                    for e in range(4):
                        row_send(q, 16 + e)

                @pl.when(core == 1)
                def _():
                    relay_copy(q).start()

            else:
                for e in range(4):
                    if i + e > 0:
                        row_send(q, 4 * i + e)
        if piece == 3:
            came[q][0] = going[0, q]

    def row_wait(q):
        block = came[q].at[1:32]
        pltpu.make_async_copy(block, block, row_sem.at[q]).wait()

    def ladder():
        loads[7].wait()
        loads[8].wait()

        def one(u, carry):
            first = pair[amp_ref[0, u], int_ref[0, u]]
            out[u] = first + pair[amp_ref[1, u], int_ref[1, u]]
            return carry

        lax.fori_loop(0, 32, one, 0, unroll=4)

    def finish(chunks):
        for q in chunks:
            row_wait(q)

        def one(u, carry):
            k = origin[0, u]
            tiles = {q: came[q][k] for q in chunks}
            for a in range(4):
                rows = slice(16 * a, 16 * a + 16)
                mixed = jnp.zeros((16, 128), jnp.float32)
                for q in chunks:
                    mixed = jnp.where(lane_block == (a + q) % 4, tiles[q], mixed)
                out[u, rows, :] += shifted(mixed, -a)
            return carry

        lax.fori_loop(0, 32, one, 0, unroll=4)

    tasks = []
    ready = []
    for q in range(NQ):
        tasks.append((START[q], functools.partial(inject, q)))
        at = {m: START[q] + DELAY[q] + t for m, t in (RING_AT if TREES[q] is RING else NEAR_AT).items()}
        for m, t in at.items():
            tasks.append((t, functools.partial(hop, q, m)))
        ready.append(max([max(at.values()) + 1.0] + [t + 4 * PIECE for t in ready]))
        tasks.append((ready[q], functools.partial(others, q)))
        for piece in range(4):
            tasks.append((ready[q] + PIECE * piece, functools.partial(products, q, piece)))
        tasks.append((ready[q] + 3.0 * PIECE + 0.1, functools.partial(relay, q)))
    tasks += [
        (0.2, send_slots),
        (1.0, indices),
        (3.51, prepare_ints),
        (5.51, ladder_pairs),
        (7.01, ladder),
        (9.01, arrivals),
        (ready[3] + 4 * PIECE, functools.partial(finish, (0, 1, 2))),
        (ready[3] + 5 * PIECE, functools.partial(finish, (3,))),
    ]
    for _, task in sorted(tasks, key=lambda entry: entry[0]):
        task()

    for q in range(NQ):
        sends = 2 * len(onward(q, 0)) + 2 * sum(0 < TREES[q][n] and n < 8 for n in TREES[q]) + 1
        await_block(q, pl.ds(0, sends), ring_sent.at[q, 0])
        await_block(q, core, ring_sent.at[q, 1])
        await_block(q, blocks(1, 8), ring_sent.at[q, 2])
        await_block(q, 16 + core, ring_sent.at[q, 3])

        @pl.when(core == 0)
        def _():
            block = going.at[1:32, q]
            pltpu.make_async_copy(block, block, row_sent.at[q]).wait()

        @pl.when(core == 1)
        def _():
            relay_copy(q).wait_send()
            pltpu.make_async_copy(passed.at[q], passed.at[q], relay_sem.at[q, 2]).wait()
            block = going.at[1:28, q]
            pltpu.make_async_copy(block, block, row_sent.at[q]).wait()

    pltpu.make_async_copy(slots.at[1:32], slots.at[1:32], slot_sent).wait()


def body(
    amp_cycle,
    cycle_ints,
    cycle_refs,
    wanted,
    cycle_dest,
    ladder_ints,
    ladder_amps,
    ladder_int_ref,
    ladder_amp_ref,
):
    operands = (
        amp_cycle,
        cycle_ints,
        cycle_refs.T,
        wanted.reshape(1, 32),
        cycle_dest,
        ladder_ints,
        ladder_amps,
        ladder_int_ref.T,
        ladder_amp_ref.T,
    )
    f32, i32 = jnp.float32, jnp.int32
    hbm = pl.BlockSpec(memory_space=pltpu.HBM)
    dma = pltpu.SemaphoreType.DMA
    return pl.pallas_call(
        kernel,
        out_shape=jax.ShapeDtypeStruct((32, 64, 128), f32),
        in_specs=[hbm] * 9,
        out_specs=pl.BlockSpec(memory_space=pltpu.VMEM),
        scratch_shapes=[
            pltpu.SMEM((2, 32), i32),
            pltpu.SMEM((1, 32), i32),
            pltpu.SMEM((32,), i32),
            pltpu.SMEM((2, 32), i32),
            pltpu.SMEM((2, 32), i32),
            pltpu.VMEM((4, 64, 128), f32),
            pltpu.VMEM((32, 2, 64, 64), f32),
            pltpu.VMEM((8, 64, 64), f32),
            pltpu.VMEM((8, 64, 128), f32),
            *[pltpu.VMEM((36, 4, 16, 128), f32)] * NQ,
            pltpu.VMEM((32, 64, 256), jnp.bfloat16),
            pltpu.VMEM((32, NQ, 16, 128), f32),
            *[pltpu.VMEM((32, 16, 128), f32)] * NQ,
            pltpu.VMEM((NQ, NX, 16, 128), f32),
            pltpu.VMEM((8, 8, 64, 128), f32),
            pltpu.VMEM((32, 128), i32),
            pltpu.VMEM((1, 128), i32),
            pltpu.VMEM((32, 128), i32),
            pltpu.VMEM((8, 128), i32),
            pltpu.SMEM((1, 128), i32),
            pltpu.SMEM((1, 128), i32),
            pltpu.SMEM((64,), i32),
            pltpu.SMEM((64,), i32),
            dma((9,)),
            dma,
            dma((NQ, 9, 2)),
            dma((NQ, 4)),
            dma((NQ, 3)),
            dma((NQ, 3)),
            dma,
            dma,
            dma((NQ,)),
            dma((NQ,)),
        ],
        compiler_params=pltpu.CompilerParams(
            collective_id=0, has_side_effects=True, vmem_limit_bytes=62 << 20
        ),
        name="cycle_and_ladder",
    )(*operands)


def solution(mesh):
    both = ("row", "col")
    placed = (
        P(both, None, None),
        P(both, None, None, None),
        P(both, None),
        P(both, None, None),
        P(both),
        P(both, None, None),
        P(both, None, None),
        P(both, None),
        P(both, None),
    )
    return jax.shard_map(
        body, mesh=mesh, in_specs=placed, out_specs=P(both, None, None), check_vma=False
    )
```

```python
import functools

import jax
import jax.numpy as jnp
from jax import lax
from jax.experimental import pallas as pl
from jax.experimental.pallas import tpu as pltpu
from jax.sharding import PartitionSpec as P

MESH = pl.DeviceIdType.MESH
NX, NY, NZ, NCORE = 4, 8, 16, 2
NQ = 4
TREES = (
    {1: 0, 2: 1, 3: 0, 4: 3, 5: 4, 6: 3, 7: 6, 8: 6},
    {1: 0, 2: 1, 3: 2, 4: 0, 5: 4, 6: 5, 7: 6, 8: 7},
    {1: 0, 2: 1, 3: 2, 4: 3, 5: 4, 6: 5, 7: 6, 8: 7},
    {1: 0, 2: 1, 3: 0, 4: 3, 5: 4, 6: 3, 7: 6, 8: 6},
)

(INJECT, HOP, GATHERED, MULTIPLY, SLOTS, INDICES, INTS, PAIRS, LADDER, ORIGINS, FINISH) = range(11)
STEPS = (
    (INJECT, 0), (INJECT, 2), (SLOTS,), (INJECT, 1), (INDICES,), (INTS,), (HOP, 0, 1),
    (HOP, 2, 1), (PAIRS,), (HOP, 1, 1), (HOP, 0, 3), (LADDER,), (ORIGINS,), (HOP, 0, 2),
    (HOP, 2, 2), (HOP, 1, 4), (HOP, 1, 2), (HOP, 0, 4), (HOP, 2, 3), (HOP, 1, 5), (HOP, 0, 6),
    (HOP, 1, 3), (HOP, 0, 5), (HOP, 2, 4), (HOP, 1, 6), (INJECT, 3), (HOP, 0, 7), (HOP, 0, 8),
    (HOP, 2, 5), (GATHERED, 0), (MULTIPLY, 0, 0), (HOP, 1, 7), (MULTIPLY, 0, 1),
    (MULTIPLY, 0, 2), (HOP, 3, 1), (MULTIPLY, 0, 3), (HOP, 2, 6), (HOP, 3, 3), (HOP, 1, 8),
    (HOP, 3, 2), (GATHERED, 1), (MULTIPLY, 1, 0), (HOP, 2, 7), (MULTIPLY, 1, 1),
    (MULTIPLY, 1, 2), (HOP, 3, 4), (MULTIPLY, 1, 3), (HOP, 3, 6), (HOP, 2, 8), (GATHERED, 2),
    (MULTIPLY, 2, 0), (HOP, 3, 5), (MULTIPLY, 2, 1), (MULTIPLY, 2, 2), (HOP, 3, 7), (HOP, 3, 8),
    (MULTIPLY, 2, 3), (GATHERED, 3), (MULTIPLY, 3, 0), (MULTIPLY, 3, 1), (MULTIPLY, 3, 2),
    (MULTIPLY, 3, 3), (FINISH, (0, 1, 2)), (FINISH, (3,)),
)

ORDER = (4, 3, 5, 2, 6, 1, 7, 0)


def shifted(value, blocks):
    amount = (blocks * 32) % 128
    return value if amount == 0 else pltpu.roll(value, amount, axis=1)


def pick(lane_block, choices):
    out = choices[0]
    for p in range(1, 4):
        out = jnp.where(lane_block == p, choices[p], out)
    return out


def split(value):
    high = value.astype(jnp.bfloat16)
    low = (value - high.astype(jnp.float32)).astype(jnp.bfloat16)
    return high, low


def kernel(
    amp_hbm,
    ints_hbm,
    refs_hbm,
    wanted_hbm,
    dest_hbm,
    lint_hbm,
    lamp_hbm,
    int_ref_hbm,
    amp_ref_hbm,
    out,
    refs,
    wanted,
    dest,
    int_ref,
    amp_ref,
    amp,
    ints,
    lint,
    lamp,
    held_0,
    held_1,
    held_2,
    held_3,
    lhs,
    going,
    came_0,
    came_1,
    came_2,
    came_3,
    pair,
    dest_col,
    slot_row,
    slots,
    table,
    inverse,
    origin,
    place,
    which,
    load_sem,
    table_sem,
    ring_sem,
    ring_sent,
    twin_sem,
    slot_sem,
    slot_sent,
    row_sem,
    row_sent,
):
    came = (came_0, came_1, came_2, came_3)
    held = (held_0, held_1, held_2, held_3)
    row, col = lax.axis_index("row"), lax.axis_index("col")
    x, y = row // NY, row % NY
    z, core = col // NCORE, col % NCORE
    way = 1 - 2 * core
    mate = 1 - core

    def along(links, to_core):
        return (row, ((z + way * links + NZ) % NZ) * NCORE + to_core)

    twin = along(0, mate)

    def peer_row(k):
        return ((x + k % NX) % NX) * NY + (y + k // NX) % NY

    loads = [
        pltpu.make_async_copy(a, b, load_sem.at[i])
        for i, (a, b) in enumerate(
            (
                (amp_hbm, amp),
                (dest_hbm, dest),
                (refs_hbm, refs),
                (wanted_hbm, wanted),
                (ints_hbm, ints),
                (lint_hbm, lint),
                (lamp_hbm, lamp),
                (int_ref_hbm, int_ref),
                (amp_ref_hbm, amp_ref),
            )
        )
    ]
    for load in loads:
        load.start()

    barrier = pltpu.get_barrier_semaphore()
    def greet(device):
        pl.semaphore_signal(barrier, inc=1, device_id=device, device_id_type=MESH)

    def greet_rows(first, last):
        def one(k, carry):
            greet((peer_row((k + 16) % 32), col))
            return carry

        lax.fori_loop(first, last, one, 0)

    starts = sorted({n for tree in TREES for n in tree if tree[n] == 0})
    strides = sorted({n - tree[n] for tree in TREES for n in tree})
    senders = [along(-links, core) for links in strides]
    senders += [along(-links, mate) for links in starts] + [twin]
    greet_rows(0, 16)
    for device in senders:
        greet(device)
    greet_rows(17, 32)

    lane_block = lax.broadcasted_iota(jnp.int32, (16, 128), 1) // 32

    loads[0].wait()
    for w in range(4):
        skewed = [shifted(amp[w, 16 * a : 16 * a + 16, :], a) for a in range(4)]
        for q in range(NQ):
            held[q][core, w] = pick(lane_block, [skewed[(p - q) % 4] for p in range(4)])

    loads[1].wait()
    for t in range(32):
        dest_col[t : t + 1, :] = jnp.full((1, 128), dest[t], jnp.int32)
    lane = lax.broadcasted_iota(jnp.int32, (32, 128), 1)
    sub = lax.broadcasted_iota(jnp.int32, (32, 128), 0)
    goal = dest_col[...]
    to_row = (goal // 32) == lane
    table[0:1, :] = jnp.max(jnp.where(to_row, sub, 0), axis=0, keepdims=True)
    slot = jnp.max(jnp.where(to_row, goal % 32, 0), axis=0, keepdims=True)
    slot_row[...] = slot
    slots[0:1, :] = slot
    invert = pltpu.make_async_copy(table.at[0:1], inverse, table_sem)
    invert.start()

    pl.semaphore_wait(barrier, len(senders) + 31)

    def send(q, source, target, device, semaphore, sent=0):
        pltpu.make_async_remote_copy(
            src_ref=held[q].at[source],
            dst_ref=held[q].at[target],
            send_sem=ring_sent.at[q, sent],
            recv_sem=semaphore,
            device_id=device,
            device_id_type=MESH,
        ).start()

    def await_block(q, block, semaphore):
        ref = held[q].at[block]
        pltpu.make_async_copy(ref, ref, semaphore).wait()

    def blocks(first, last):
        return pl.ds(2 * first, 2 * (last - first))

    def onward(q, m):
        return sorted((n for n in TREES[q] if TREES[q][n] == m), reverse=True)

    def inject(q):
        for n in onward(q, 0):
            send(q, core, 2 * n + core, along(n, core), ring_sem.at[q, n, core])
            send(q, core, 2 * n + core, along(-n, mate), ring_sem.at[q, n, core])
        send(q, core, core, twin, twin_sem.at[q, 0], sent=1)

    def hop(q, m):
        if TREES[q][m] == 0:
            for c in range(NCORE):
                await_block(q, 2 * m + c, ring_sem.at[q, m, c])
        elif m < 8:
            await_block(q, blocks(m, m + 1), ring_sem.at[q, m, 0])
        else:
            await_block(q, 16 + core, ring_sem.at[q, 8, 0])
        for n in onward(q, m):
            if n == 8:
                send(q, 2 * m + core, 16 + core, along(8 - m, core), ring_sem.at[q, 8, 0])
            else:
                send(q, blocks(m, m + 1), blocks(n, n + 1), along(n - m, core), ring_sem.at[q, n, 0])
        if m == 8:
            send(q, 16 + core, 34 + core, twin, twin_sem.at[q, 2], sent=3)
        else:
            send(q, blocks(m, m + 1), blocks(m + 9, m + 10), twin, twin_sem.at[q, 1], sent=2)

    def others(q):
        await_block(q, mate, twin_sem.at[q, 0])
        await_block(q, blocks(10, 17), twin_sem.at[q, 1])
        await_block(q, 34 + mate, twin_sem.at[q, 2])

    def send_slots():
        def one(k, carry):
            pltpu.make_async_remote_copy(
                src_ref=slot_row,
                dst_ref=slots.at[pl.ds(k, 1)],
                send_sem=slot_sent,
                recv_sem=slot_sem,
                device_id=(peer_row(k), col),
                device_id_type=MESH,
            ).start()
            return carry

        lax.fori_loop(1, 32, one, 0)

    def indices():
        invert.wait()
        loads[2].wait()
        loads[3].wait()

        def one(k, carry):
            t = inverse[0, peer_row(k)]
            for s in range(2):
                h = refs[s, t]
                m = (way * (z - h // 2) + 2 * NZ) % NZ
                own = jnp.logical_or(m < 8, jnp.logical_and(m == 8, h % 2 == core))
                place[2 * k + s] = jnp.where(own, 2 * m, 18 + 2 * (NZ - m)) + h % 2
                which[2 * k + s] = wanted[0, h]
            return carry

        lax.fori_loop(0, 32, one, 0, unroll=4)

    def prepare_ints():
        loads[4].wait()

        def one(k, carry):
            t = inverse[0, peer_row(k)]
            both = jnp.concatenate([ints[t, 0], ints[t, 1]], axis=1)
            high, low = split(both)
            lhs[k] = jnp.concatenate([high, low], axis=1)
            return carry

        lax.fori_loop(0, 32, one, 0, unroll=4)

    def ladder_pairs():
        loads[5].wait()
        loads[6].wait()
        ih, il = split(lint[...].reshape(512, 64))
        left = jnp.concatenate([ih, il, ih], axis=1)

        def one(b, carry):
            high, low = split(lamp[b])
            right = jnp.concatenate([high, high, low], axis=0)
            product = jnp.dot(left, right, preferred_element_type=jnp.float32)
            pair[b] = product.reshape(8, 64, 128)
            return carry

        lax.fori_loop(0, 8, one, 0, unroll=2)

    def arrivals():
        pltpu.make_async_copy(slots.at[1:32], slots.at[1:32], slot_sem).wait()
        mine = jnp.max(jnp.where(lane == row, slots[...], 0), axis=1, keepdims=True)
        table[1:2, :] = jnp.max(jnp.where(mine == lane, sub, 0), axis=0, keepdims=True)
        copy = pltpu.make_async_copy(table.at[1:2], origin, table_sem)
        copy.start()
        copy.wait()

    def chunk_products(q, i):
        rows = []
        for s in range(2):
            turned = [
                shifted(held[q][place[8 * i + 2 * e + s], which[8 * i + 2 * e + s]], e)
                for e in range(4)
            ]
            for a in range(4):
                mixed = pick(lane_block, [turned[(p - a - q) % 4] for p in range(4)])
                rows.append(shifted(mixed, -a - q))
        high, low = split(jnp.concatenate(rows, axis=0))
        left = lhs[pl.ds(4 * i, 4)].reshape(256, 256)
        product = jnp.dot(
            left, jnp.concatenate([high, high], axis=0), preferred_element_type=jnp.float32
        ) + jnp.dot(left[:, :128], low, preferred_element_type=jnp.float32)
        for e in range(4):
            parts = [
                shifted(product[64 * e + 16 * a : 64 * e + 16 * a + 16, :], a) for a in range(4)
            ]
            mixed = pick(lane_block, [parts[(p - e) % 4] for p in range(4)])
            going[4 * i + e, q] = shifted(mixed, q - e)

    def row_send(q, k):
        pltpu.make_async_remote_copy(
            src_ref=going.at[k, q],
            dst_ref=came[q].at[k],
            send_sem=row_sent.at[q],
            recv_sem=row_sem.at[q],
            device_id=(peer_row(k), col),
            device_id_type=MESH,
        ).start()

    def products(q, piece):
        for i in ORDER[2 * piece : 2 * piece + 2]:
            chunk_products(q, i)
        for i in ORDER[2 * piece : 2 * piece + 2]:
            for e in range(4):
                if i + e > 0:
                    row_send(q, 4 * i + e)
        if piece == 3:
            came[q][0] = going[0, q]

    def row_wait(q):
        block = came[q].at[1:32]
        pltpu.make_async_copy(block, block, row_sem.at[q]).wait()

    def ladder():
        loads[7].wait()
        loads[8].wait()

        def one(u, carry):
            first = pair[amp_ref[0, u], int_ref[0, u]]
            out[u] = first + pair[amp_ref[1, u], int_ref[1, u]]
            return carry

        lax.fori_loop(0, 32, one, 0, unroll=4)

    def finish(chunks):
        for q in chunks:
            row_wait(q)

        def one(u, carry):
            k = origin[0, u]
            tiles = {q: came[q][k] for q in chunks}
            for a in range(4):
                rows = slice(16 * a, 16 * a + 16)
                mixed = jnp.zeros((16, 128), jnp.float32)
                for q in chunks:
                    mixed = jnp.where(lane_block == (a + q) % 4, tiles[q], mixed)
                out[u, rows, :] += shifted(mixed, -a)
            return carry

        lax.fori_loop(0, 32, one, 0, unroll=4)

    acts = {
        INJECT: inject,
        HOP: hop,
        GATHERED: others,
        MULTIPLY: products,
        SLOTS: send_slots,
        INDICES: indices,
        INTS: prepare_ints,
        PAIRS: ladder_pairs,
        LADDER: ladder,
        ORIGINS: arrivals,
        FINISH: lambda *chunks: finish(chunks[0]),
    }
    for act, *details in STEPS:
        acts[act](*details)

    for q in range(NQ):
        sends = 2 * len(onward(q, 0)) + 2 * sum(0 < TREES[q][n] and n < 8 for n in TREES[q]) + 1
        await_block(q, pl.ds(0, sends), ring_sent.at[q, 0])
        await_block(q, core, ring_sent.at[q, 1])
        await_block(q, blocks(1, 8), ring_sent.at[q, 2])
        await_block(q, 16 + core, ring_sent.at[q, 3])

        block = going.at[1:32, q]
        pltpu.make_async_copy(block, block, row_sent.at[q]).wait()

    pltpu.make_async_copy(slots.at[1:32], slots.at[1:32], slot_sent).wait()


def body(
    amp_cycle,
    cycle_ints,
    cycle_refs,
    wanted,
    cycle_dest,
    ladder_ints,
    ladder_amps,
    ladder_int_ref,
    ladder_amp_ref,
):
    operands = (
        amp_cycle,
        cycle_ints,
        cycle_refs.T,
        wanted.reshape(1, 32),
        cycle_dest,
        ladder_ints,
        ladder_amps,
        ladder_int_ref.T,
        ladder_amp_ref.T,
    )
    f32, i32 = jnp.float32, jnp.int32
    hbm = pl.BlockSpec(memory_space=pltpu.HBM)
    dma = pltpu.SemaphoreType.DMA
    return pl.pallas_call(
        kernel,
        out_shape=jax.ShapeDtypeStruct((32, 64, 128), f32),
        in_specs=[hbm] * 9,
        out_specs=pl.BlockSpec(memory_space=pltpu.VMEM),
        scratch_shapes=[
            pltpu.SMEM((2, 32), i32),
            pltpu.SMEM((1, 32), i32),
            pltpu.SMEM((32,), i32),
            pltpu.SMEM((2, 32), i32),
            pltpu.SMEM((2, 32), i32),
            pltpu.VMEM((4, 64, 128), f32),
            pltpu.VMEM((32, 2, 64, 64), f32),
            pltpu.VMEM((8, 64, 64), f32),
            pltpu.VMEM((8, 64, 128), f32),
            *[pltpu.VMEM((36, 4, 16, 128), f32)] * NQ,
            pltpu.VMEM((32, 64, 256), jnp.bfloat16),
            pltpu.VMEM((32, NQ, 16, 128), f32),
            *[pltpu.VMEM((32, 16, 128), f32)] * NQ,
            pltpu.VMEM((8, 8, 64, 128), f32),
            pltpu.VMEM((32, 128), i32),
            pltpu.VMEM((1, 128), i32),
            pltpu.VMEM((32, 128), i32),
            pltpu.VMEM((8, 128), i32),
            pltpu.SMEM((1, 128), i32),
            pltpu.SMEM((1, 128), i32),
            pltpu.SMEM((64,), i32),
            pltpu.SMEM((64,), i32),
            dma((9,)),
            dma,
            dma((NQ, 9, 2)),
            dma((NQ, 4)),
            dma((NQ, 3)),
            dma,
            dma,
            dma((NQ,)),
            dma((NQ,)),
        ],
        compiler_params=pltpu.CompilerParams(
            collective_id=0, has_side_effects=True, vmem_limit_bytes=40 << 20
        ),
        name="cycle_and_ladder",
    )(*(pltpu.with_memory_space_constraint(v, pltpu.HBM) for v in operands))


def solution(mesh):
    both = ("row", "col")
    placed = (
        P(both, None, None),
        P(both, None, None, None),
        P(both, None),
        P(both, None, None),
        P(both),
        P(both, None, None),
        P(both, None, None),
        P(both, None),
        P(both, None),
    )
    return jax.shard_map(
        body, mesh=mesh, in_specs=placed, out_specs=P(both, None, None), check_vma=False
    )
```

```python
import functools

import jax
import jax.numpy as jnp
from jax import lax
from jax.experimental import pallas as pl
from jax.experimental.pallas import tpu as pltpu
from jax.sharding import PartitionSpec as P

MESH = pl.DeviceIdType.MESH
NX, NY, NZ, NCORE = 4, 8, 16, 2
NQ = 4
TREES = (
    {1: 0, 2: 1, 3: 2, 4: 3, 5: 4, 6: 5, 7: 6, 8: 7},
    {1: 0, 2: 0, 3: 2, 4: 2, 5: 4, 6: 4, 7: 6, 8: 6},
    {1: 0, 2: 0, 3: 2, 4: 2, 5: 4, 6: 4, 7: 6, 8: 6},
    {1: 0, 2: 1, 3: 0, 4: 3, 5: 4, 6: 3, 7: 6, 8: 6},
)

(INJECT, HOP, GATHERED, MULTIPLY, SLOTS, INDICES, INTS, PAIRS, LADDER, ORIGINS, FINISH) = range(11)
STEPS = (
    (INJECT, 0), (INJECT, 2), (INDICES,), (INJECT, 1), (INTS, 0), (INTS, 1), (INTS, 2),
    (HOP, 0, 1), (INTS, 3), (INTS, 4), (INTS, 5), (HOP, 2, 1), (INTS, 6), (HOP, 2, 2),
    (INTS, 7), (SLOTS, 0), (HOP, 1, 1), (SLOTS, 1), (HOP, 0, 2), (HOP, 1, 2), (SLOTS, 2),
    (SLOTS, 3), (HOP, 2, 3), (HOP, 2, 4), (HOP, 0, 3), (HOP, 1, 3), (HOP, 1, 4), (HOP, 2, 5),
    (HOP, 0, 4), (HOP, 2, 6), (HOP, 1, 5), (INJECT, 3), (HOP, 1, 6), (HOP, 0, 5), (HOP, 2, 7),
    (HOP, 2, 8), (GATHERED, 2), (MULTIPLY, 2, 0), (HOP, 3, 1), (MULTIPLY, 2, 1), (HOP, 1, 7),
    (MULTIPLY, 2, 2), (HOP, 0, 6), (HOP, 1, 8), (MULTIPLY, 2, 3), (HOP, 3, 3), (HOP, 3, 2),
    (GATHERED, 1), (MULTIPLY, 1, 0), (MULTIPLY, 1, 1), (HOP, 0, 7), (MULTIPLY, 1, 2),
    (MULTIPLY, 1, 3), (HOP, 3, 4), (HOP, 3, 6), (HOP, 0, 8), (GATHERED, 0), (MULTIPLY, 0, 0),
    (HOP, 3, 5), (MULTIPLY, 0, 1), (MULTIPLY, 0, 2), (HOP, 3, 7), (HOP, 3, 8), (MULTIPLY, 0, 3),
    (GATHERED, 3), (MULTIPLY, 3, 0), (MULTIPLY, 3, 1), (MULTIPLY, 3, 2), (MULTIPLY, 3, 3),
    (PAIRS,), (LADDER,), (ORIGINS,), (FINISH, (0, 1, 2)), (FINISH, (3,)),
)

ORDER = (4, 3, 5, 2, 6, 1, 7, 0)


def shifted(value, blocks):
    amount = (blocks * 32) % 128
    return value if amount == 0 else pltpu.roll(value, amount, axis=1)


def pick(lane_block, choices):
    out = choices[0]
    for p in range(1, 4):
        out = jnp.where(lane_block == p, choices[p], out)
    return out


def split(value):
    high = value.astype(jnp.bfloat16)
    low = (value - high.astype(jnp.float32)).astype(jnp.bfloat16)
    return high, low


def kernel(
    amp_hbm,
    ints_hbm,
    refs_hbm,
    wanted_hbm,
    dest_hbm,
    lint_hbm,
    lamp_hbm,
    int_ref_hbm,
    amp_ref_hbm,
    out,
    refs,
    wanted,
    dest,
    int_ref,
    amp_ref,
    amp,
    ints,
    lint,
    lamp,
    held_0,
    held_1,
    held_2,
    held_3,
    lhs,
    going,
    came_0,
    came_1,
    came_2,
    came_3,
    pair,
    dest_col,
    slot_row,
    slots,
    table,
    inverse,
    origin,
    place,
    which,
    load_sem,
    table_sem,
    ring_sem,
    ring_sent,
    twin_sem,
    slot_sem,
    slot_sent,
    row_sem,
    row_sent,
):
    came = (came_0, came_1, came_2, came_3)
    held = (held_0, held_1, held_2, held_3)
    row, col = lax.axis_index("row"), lax.axis_index("col")
    x, y = row // NY, row % NY
    z, core = col // NCORE, col % NCORE
    way = 1 - 2 * core
    mate = 1 - core

    def along(links, to_core):
        return (row, ((z + way * links + NZ) % NZ) * NCORE + to_core)

    twin = along(0, mate)

    def peer_row(k):
        return ((x + k % NX) % NX) * NY + (y + k // NX) % NY

    loads = [
        pltpu.make_async_copy(a, b, load_sem.at[i])
        for i, (a, b) in enumerate(
            (
                (amp_hbm, amp),
                (dest_hbm, dest),
                (refs_hbm, refs),
                (wanted_hbm, wanted),
                (ints_hbm, ints),
                (lint_hbm, lint),
                (lamp_hbm, lamp),
                (int_ref_hbm, int_ref),
                (amp_ref_hbm, amp_ref),
            )
        )
    ]
    for load in loads:
        load.start()

    barrier = pltpu.get_barrier_semaphore()
    def greet(device):
        pl.semaphore_signal(barrier, inc=1, device_id=device, device_id_type=MESH)

    def greet_rows(first, last):
        def one(k, carry):
            greet((peer_row((k + 16) % 32), col))
            return carry

        lax.fori_loop(first, last, one, 0)

    starts = sorted({n for tree in TREES for n in tree if tree[n] == 0})
    strides = sorted({n - tree[n] for tree in TREES for n in tree})
    senders = [along(-links, core) for links in strides]
    senders += [along(-links, mate) for links in starts] + [twin]
    greet_rows(0, 16)
    for device in senders:
        greet(device)
    greet_rows(17, 32)

    lane_block = lax.broadcasted_iota(jnp.int32, (16, 128), 1) // 32

    loads[0].wait()
    for w in range(4):
        skewed = [shifted(amp[w, 16 * a : 16 * a + 16, :], a) for a in range(4)]
        for q in range(NQ):
            held[q][core, w] = pick(lane_block, [skewed[(p - q) % 4] for p in range(4)])

    loads[1].wait()
    for t in range(32):
        dest_col[t : t + 1, :] = jnp.full((1, 128), dest[t], jnp.int32)
    lane = lax.broadcasted_iota(jnp.int32, (32, 128), 1)
    sub = lax.broadcasted_iota(jnp.int32, (32, 128), 0)
    goal = dest_col[...]
    to_row = (goal // 32) == lane
    table[0:1, :] = jnp.max(jnp.where(to_row, sub, 0), axis=0, keepdims=True)
    slot = jnp.max(jnp.where(to_row, goal % 32, 0), axis=0, keepdims=True)
    slot_row[...] = slot
    slots[0:1, :] = slot
    invert = pltpu.make_async_copy(table.at[0:1], inverse, table_sem)
    invert.start()

    pl.semaphore_wait(barrier, len(senders) + 31)

    def send(q, source, target, device, semaphore, sent=0):
        pltpu.make_async_remote_copy(
            src_ref=held[q].at[source],
            dst_ref=held[q].at[target],
            send_sem=ring_sent.at[q, sent],
            recv_sem=semaphore,
            device_id=device,
            device_id_type=MESH,
        ).start()

    def await_block(q, block, semaphore):
        ref = held[q].at[block]
        pltpu.make_async_copy(ref, ref, semaphore).wait()

    def blocks(first, last):
        return pl.ds(2 * first, 2 * (last - first))

    def onward(q, m):
        return sorted((n for n in TREES[q] if TREES[q][n] == m), reverse=True)

    def inject(q):
        for n in onward(q, 0):
            send(q, core, 2 * n + core, along(n, core), ring_sem.at[q, n, core])
            send(q, core, 2 * n + core, along(-n, mate), ring_sem.at[q, n, core])
        send(q, core, core, twin, twin_sem.at[q, 0], sent=1)

    def hop(q, m):
        if TREES[q][m] == 0:
            for c in range(NCORE):
                await_block(q, 2 * m + c, ring_sem.at[q, m, c])
        elif m < 8:
            await_block(q, blocks(m, m + 1), ring_sem.at[q, m, 0])
        else:
            await_block(q, 16 + core, ring_sem.at[q, 8, 0])
        for n in onward(q, m):
            if n == 8:
                send(q, 2 * m + core, 16 + core, along(8 - m, core), ring_sem.at[q, 8, 0])
            else:
                send(q, blocks(m, m + 1), blocks(n, n + 1), along(n - m, core), ring_sem.at[q, n, 0])
        if m == 8:
            send(q, 16 + core, 34 + core, twin, twin_sem.at[q, 2], sent=3)
        else:
            send(q, blocks(m, m + 1), blocks(m + 9, m + 10), twin, twin_sem.at[q, 1], sent=2)

    def others(q):
        await_block(q, mate, twin_sem.at[q, 0])
        await_block(q, blocks(10, 17), twin_sem.at[q, 1])
        await_block(q, 34 + mate, twin_sem.at[q, 2])

    def send_slots(part):
        for k in range(max(1, 8 * part), 8 * part + 8):
            pltpu.make_async_remote_copy(
                src_ref=slot_row,
                dst_ref=slots.at[pl.ds(k, 1)],
                send_sem=slot_sent,
                recv_sem=slot_sem,
                device_id=(peer_row(k), col),
                device_id_type=MESH,
            ).start()

    def indices():
        invert.wait()
        loads[2].wait()
        loads[3].wait()

        def one(k, carry):
            t = inverse[0, peer_row(k)]
            for s in range(2):
                h = refs[s, t]
                m = (way * (z - h // 2) + 2 * NZ) % NZ
                own = jnp.logical_or(m < 8, jnp.logical_and(m == 8, h % 2 == core))
                place[2 * k + s] = jnp.where(own, 2 * m, 18 + 2 * (NZ - m)) + h % 2
                which[2 * k + s] = wanted[0, h]
            return carry

        lax.fori_loop(0, 32, one, 0, unroll=4)

    def prepare_ints(part):
        if part == 0:
            loads[4].wait()
        for k in range(4 * part, 4 * part + 4):
            t = inverse[0, peer_row(k)]
            both = jnp.concatenate([ints[t, 0], ints[t, 1]], axis=1)
            high, low = split(both)
            lhs[k] = jnp.concatenate([high, low], axis=1)

    def ladder_pairs():
        loads[5].wait()
        loads[6].wait()
        ih, il = split(lint[...].reshape(512, 64))
        left = jnp.concatenate([ih, il, ih], axis=1)

        def one(b, carry):
            high, low = split(lamp[b])
            right = jnp.concatenate([high, high, low], axis=0)
            product = jnp.dot(left, right, preferred_element_type=jnp.float32)
            pair[b] = product.reshape(8, 64, 128)
            return carry

        lax.fori_loop(0, 8, one, 0, unroll=2)

    def arrivals():
        pltpu.make_async_copy(slots.at[1:32], slots.at[1:32], slot_sem).wait()
        mine = jnp.max(jnp.where(lane == row, slots[...], 0), axis=1, keepdims=True)
        table[1:2, :] = jnp.max(jnp.where(mine == lane, sub, 0), axis=0, keepdims=True)
        copy = pltpu.make_async_copy(table.at[1:2], origin, table_sem)
        copy.start()
        copy.wait()

    def chunk_products(q, i):
        rows = []
        for s in range(2):
            turned = [
                shifted(held[q][place[8 * i + 2 * e + s], which[8 * i + 2 * e + s]], e)
                for e in range(4)
            ]
            for a in range(4):
                mixed = pick(lane_block, [turned[(p - a - q) % 4] for p in range(4)])
                rows.append(shifted(mixed, -a - q))
        high, low = split(jnp.concatenate(rows, axis=0))
        left = lhs[pl.ds(4 * i, 4)].reshape(256, 256)
        product = jnp.dot(
            left, jnp.concatenate([high, high], axis=0), preferred_element_type=jnp.float32
        ) + jnp.dot(left[:, :128], low, preferred_element_type=jnp.float32)
        for e in range(4):
            parts = [
                shifted(product[64 * e + 16 * a : 64 * e + 16 * a + 16, :], a) for a in range(4)
            ]
            mixed = pick(lane_block, [parts[(p - e) % 4] for p in range(4)])
            going[4 * i + e, q] = shifted(mixed, q - e)

    def row_send(q, k):
        pltpu.make_async_remote_copy(
            src_ref=going.at[k, q],
            dst_ref=came[q].at[k],
            send_sem=row_sent.at[q],
            recv_sem=row_sem.at[q],
            device_id=(peer_row(k), col),
            device_id_type=MESH,
        ).start()

    def products(q, piece):
        for i in ORDER[2 * piece : 2 * piece + 2]:
            chunk_products(q, i)
        for i in ORDER[2 * piece : 2 * piece + 2]:
            for e in range(4):
                if i + e > 0:
                    row_send(q, 4 * i + e)
        if piece == 3:
            came[q][0] = going[0, q]

    def row_wait(q):
        block = came[q].at[1:32]
        pltpu.make_async_copy(block, block, row_sem.at[q]).wait()

    def ladder():
        loads[7].wait()
        loads[8].wait()

        def one(u, carry):
            first = pair[amp_ref[0, u], int_ref[0, u]]
            out[u] = first + pair[amp_ref[1, u], int_ref[1, u]]
            return carry

        lax.fori_loop(0, 32, one, 0, unroll=4)

    def finish(chunks):
        for q in chunks:
            row_wait(q)

        def one(u, carry):
            k = origin[0, u]
            tiles = {q: came[q][k] for q in chunks}
            for a in range(4):
                rows = slice(16 * a, 16 * a + 16)
                mixed = jnp.zeros((16, 128), jnp.float32)
                for q in chunks:
                    mixed = jnp.where(lane_block == (a + q) % 4, tiles[q], mixed)
                out[u, rows, :] += shifted(mixed, -a)
            return carry

        lax.fori_loop(0, 32, one, 0, unroll=4)

    acts = {
        INJECT: inject,
        HOP: hop,
        GATHERED: others,
        MULTIPLY: products,
        SLOTS: send_slots,
        INDICES: indices,
        INTS: prepare_ints,
        PAIRS: ladder_pairs,
        LADDER: ladder,
        ORIGINS: arrivals,
        FINISH: lambda *chunks: finish(chunks[0]),
    }
    for act, *details in STEPS:
        acts[act](*details)

    for q in range(NQ):
        sends = 2 * len(onward(q, 0)) + 2 * sum(0 < TREES[q][n] and n < 8 for n in TREES[q]) + 1
        await_block(q, pl.ds(0, sends), ring_sent.at[q, 0])
        await_block(q, core, ring_sent.at[q, 1])
        await_block(q, blocks(1, 8), ring_sent.at[q, 2])
        await_block(q, 16 + core, ring_sent.at[q, 3])

        block = going.at[1:32, q]
        pltpu.make_async_copy(block, block, row_sent.at[q]).wait()

    pltpu.make_async_copy(slots.at[1:32], slots.at[1:32], slot_sent).wait()


def body(
    amp_cycle,
    cycle_ints,
    cycle_refs,
    wanted,
    cycle_dest,
    ladder_ints,
    ladder_amps,
    ladder_int_ref,
    ladder_amp_ref,
):
    operands = (
        amp_cycle,
        cycle_ints,
        cycle_refs.T,
        wanted.reshape(1, 32),
        cycle_dest,
        ladder_ints,
        ladder_amps,
        ladder_int_ref.T,
        ladder_amp_ref.T,
    )
    f32, i32 = jnp.float32, jnp.int32
    hbm = pl.BlockSpec(memory_space=pltpu.HBM)
    dma = pltpu.SemaphoreType.DMA
    return pl.pallas_call(
        kernel,
        out_shape=jax.ShapeDtypeStruct((32, 64, 128), f32),
        in_specs=[hbm] * 9,
        out_specs=pl.BlockSpec(memory_space=pltpu.VMEM),
        scratch_shapes=[
            pltpu.SMEM((2, 32), i32),
            pltpu.SMEM((1, 32), i32),
            pltpu.SMEM((32,), i32),
            pltpu.SMEM((2, 32), i32),
            pltpu.SMEM((2, 32), i32),
            pltpu.VMEM((4, 64, 128), f32),
            pltpu.VMEM((32, 2, 64, 64), f32),
            pltpu.VMEM((8, 64, 64), f32),
            pltpu.VMEM((8, 64, 128), f32),
            *[pltpu.VMEM((36, 4, 16, 128), f32)] * NQ,
            pltpu.VMEM((32, 64, 256), jnp.bfloat16),
            pltpu.VMEM((32, NQ, 16, 128), f32),
            *[pltpu.VMEM((32, 16, 128), f32)] * NQ,
            pltpu.VMEM((8, 8, 64, 128), f32),
            pltpu.VMEM((32, 128), i32),
            pltpu.VMEM((1, 128), i32),
            pltpu.VMEM((32, 128), i32),
            pltpu.VMEM((8, 128), i32),
            pltpu.SMEM((1, 128), i32),
            pltpu.SMEM((1, 128), i32),
            pltpu.SMEM((64,), i32),
            pltpu.SMEM((64,), i32),
            dma((9,)),
            dma,
            dma((NQ, 9, 2)),
            dma((NQ, 4)),
            dma((NQ, 3)),
            dma,
            dma,
            dma((NQ,)),
            dma((NQ,)),
        ],
        compiler_params=pltpu.CompilerParams(
            collective_id=0, has_side_effects=True, vmem_limit_bytes=40 << 20
        ),
        name="cycle_and_ladder",
    )(*(pltpu.with_memory_space_constraint(v, pltpu.HBM) for v in operands))


def solution(mesh):
    both = ("row", "col")
    placed = (
        P(both, None, None),
        P(both, None, None, None),
        P(both, None),
        P(both, None, None),
        P(both),
        P(both, None, None),
        P(both, None, None),
        P(both, None),
        P(both, None),
    )
    return jax.shard_map(
        body, mesh=mesh, in_specs=placed, out_specs=P(both, None, None), check_vma=False
    )
```
